128 devices in a mesh: pp: 8 (over z, core), ep: 16 (over x, y).
Axes of the slice: x: 4, y: 4, z: 4, core: 2. Of those that a mesh axis runs over, the one named last changes fastest.
Arguments:
- inputs: bfloat16 [8, 256, 7168], P(None, 'ep'), may hold values from -16 to 16
- norm_gain: float32 [8, 7168], P('pp'), may hold values from 0.25 to 1.75
- router_weight: bfloat16 [8, 7168, 8], P('pp'), may hold values from -0.0625 to 0.0625
- gate_weight: bfloat16 [8, 7168, 8192], P('pp', None, 'ep'), may hold values from -0.0625 to 0.0625
- up_weight: bfloat16 [8, 7168, 8192], P('pp', None, 'ep'), may hold values from -0.0625 to 0.0625
- down_weight: bfloat16 [8, 1024, 57344], P('pp', None, 'ep'), may hold values from -0.1875 to 0.1875
- routing: int32 [8, 8, 256, 2], P('pp', None, 'ep'), may hold values from 0 to 7, all different within a row; in each aligned block of 16 rows (0 to 15, 16 to 31, ..., all dimensions but the last counted through in order) at most 5 rows name the same one
Outputs:
- final: bfloat16 [8, 256, 7168], P('pp', 'ep')
The draws below stay inside these ranges and needn't reach their ends.
Inputs may be any that keep to these rules, and one draw needn't show every extreme that they name: `routing`: each token names 2 different experts. Among the 16 tokens of one device in one micro-batch of one layer, no expert is named more than 5 times, and in some of these aligned blocks one expert is named exactly 5 times.
All inputs are finite; a program needn't handle non-finite values.
Results may differ from the reference program's by a relative error of at most 0.025.
Values may be sent and summed in bfloat16 or wider, within the bound.
No kernel may reach another device: no remote copies, remote signals or barrier semaphores. Data moves between devices by JAX's collectives and lax.ppermute only.
A program may use at most 128 MiB of HBM per device.

```python
import math
import jax
import jax.numpy as jnp
import numpy as np
from jax import lax

D = 7168
HID = 1024
TOPK = 2
TOK_DEV = 16
EXPERTS = 8
MOST = 5
MB = 8
LAYERS = 8
TOKENS = 256
N_EP = 16


def draw_inputs(key, part):
    key_rows = jax.random.fold_in(key, 11)
    key_values = jax.random.fold_in(key, 12)
    values = jnp.clip(jax.random.normal(key_values, (MB, TOKENS, D), jnp.float32), -4.0, 4.0)
    row_scale = jnp.exp(jax.random.uniform(key_rows, (MB, TOKENS, 1), jnp.float32, math.log(0.4), math.log(4.0)))
    return (values * row_scale).astype(jnp.bfloat16)


def level_of(rng, extent, cuts, least, high):
    level, own = 1.0, jax.random.fold_in(rng, 6)
    for position, blocks in cuts:
        draws = jnp.exp(jax.random.uniform(jax.random.fold_in(own, position), (blocks,), jnp.float32, least / len(cuts), high / len(cuts)))
        level = level * jnp.repeat(draws, extent[position] // blocks).reshape([-1 if axis == position else 1 for axis in range(len(extent))])
    return level


def shared_out(own_key, own, number, rows, number_of, top, reach, lean):
    ranking = jax.random.permutation(own_key, number_of)
    heavy_load, usual = load_shares(number_of, rows * top, reach, lean, True), load_shares(number_of, rows * top, reach, lean, False)
    places = jnp.arange(number_of)

    def named(lengths, rotation):
        used = int((lengths > 0).sum())
        fixed = max(1, used // 4)
        passed = fixed + (places - fixed + rotation * (used - fixed)) % max(1, number_of - fixed)
        return jnp.zeros((number_of,), jnp.int32).at[ranking[jnp.where(places < fixed, places, passed)]].set(jnp.asarray(lengths, jnp.int32))

    lengths = jnp.where(number % 4 == 0, named(heavy_load, number // 4), named(usual, number - number // 4 - 1))
    mixed = jax.random.permutation(jax.random.fold_in(own, 3), number_of)
    giver, sink = mixed[0:number_of // 2 * 2:2], mixed[1:number_of // 2 * 2:2]
    slack = jnp.minimum(lengths[giver] - 1, reach - lengths[sink]) // 2
    slack = jnp.where((giver == ranking[0]) | (sink == ranking[0]) | (lengths[sink] == 0), 0, jnp.maximum(slack, 0))
    passed = jax.random.randint(jax.random.fold_in(own, 4), (number_of // 2,), 0, 1 << 20) % (slack + 1)
    lengths = lengths.at[giver].add(-passed).at[sink].add(passed)
    labels = jnp.searchsorted(jnp.cumsum(lengths), jnp.arange(rows * top), side="right").astype(jnp.int32)
    listing = labels.reshape(top, rows).T
    listing = listing[jax.random.permutation(jax.random.fold_in(own, 1), rows)]
    rotation = jax.random.randint(jax.random.fold_in(own, 2), (rows, 1), 0, top)
    return jnp.take_along_axis(listing, (jnp.arange(top)[None, :] + rotation) % top, axis=1)


def load_shares(amount, total, bound, skew, full):
    loads = [(1 << 20) // math.isqrt(standing ** skew) + 1 for standing in range(1, amount + 1)]
    largest = bound if full else min(bound, max(-(-total // amount), total * loads[0] // sum(loads)))
    least = 1 if total - largest >= amount - 1 else 0
    given, spare = [largest] + [least] * (amount - 1), total - largest - least * (amount - 1)
    while spare > 0:
        free = [i for i in range(1, amount) if given[i] < largest] or [i for i in range(1, amount) if given[i] < bound]
        pool, remaining = sum([loads[i] for i in free]), spare
        for i in free:
            more = min(bound - given[i], max(1, remaining * loads[i] // pool), spare)
            given[i] = given[i] + more
            spare = spare - more
    return np.array(given)


def bell_draw(own_key, dims, scale, bound, cuts=(), kind=jnp.bfloat16):
    result = jax.random.normal(own_key, dims, jnp.float32) * scale
    if len(cuts) > 0:
        result = level_of(own_key, dims, cuts, -0.22, 0.18) * result
    return jnp.clip(result, min=-bound, max=bound).astype(kind)


def setup_inputs(seed: int = 0) -> dict:
    splits = jax.random.split(jax.random.key(seed), 8)
    inputs = draw_inputs(jax.random.fold_in(splits[7], 71), 0)
    norm_gain = jnp.clip(1.0 + 0.15 * jax.random.normal(splits[1], (LAYERS, D), jnp.float32), 0.25, 1.75)
    router_weight = bell_draw(splits[2], (LAYERS, D, EXPERTS), D ** -0.5, 0.0625, ((0, 8),))
    gate_weight = bell_draw(splits[3], (LAYERS, D, EXPERTS * HID), D ** -0.5, 0.0625, ((0, 8), (2, 16)))
    up_weight = bell_draw(splits[4], (LAYERS, D, EXPERTS * HID), D ** -0.5, 0.0625, ((0, 8), (2, 16)))
    down_weight = bell_draw(splits[5], (LAYERS, HID, EXPERTS * D), HID ** -0.5, 0.1875, ((0, 8), (2, 16)))
    routing_keys = jax.random.split(jax.random.fold_in(splits[6], 1), LAYERS * MB * TOKENS // TOK_DEV)
    routing_turns = jax.random.permutation(jax.random.fold_in(splits[6], 3), LAYERS * MB * TOKENS // TOK_DEV)
    routing = jax.vmap(lambda own, number: shared_out(jax.random.fold_in(splits[6], 2), own, number, TOK_DEV, EXPERTS, TOPK, MOST, 2))(routing_keys, routing_turns).reshape((LAYERS, MB, TOKENS, TOPK))
    return {"inputs": inputs, "norm_gain": norm_gain, "router_weight": router_weight, "gate_weight": gate_weight, "up_weight": up_weight, "down_weight": down_weight, "routing": routing}


routed_scale = 2.5
norm_epsilon = 1e-06

def expert_rows(rows, gate_block, up_block, down_block):
    gate_proj = jnp.dot(rows, gate_block, preferred_element_type=jnp.float32)
    up_proj = jnp.dot(rows, up_block, preferred_element_type=jnp.float32)
    hidden = (jax.nn.silu(gate_proj) * up_proj).astype(jnp.bfloat16)
    return jnp.dot(hidden, down_block, preferred_element_type=jnp.float32).astype(jnp.bfloat16)

def moe_layer(activations, gain_row, router, gate_all, up_all, down_all, routes):
    current = activations.astype(jnp.float32)
    mean_square = lax.optimization_barrier(jnp.mean(current * current, axis=1, keepdims=True))
    normed = (current * lax.rsqrt(mean_square + norm_epsilon) * gain_row).astype(jnp.bfloat16)
    scores = jax.nn.sigmoid(jnp.dot(normed, router, preferred_element_type=jnp.float32))
    expert_ids = jnp.arange(EXPERTS, dtype=jnp.int32)
    onehot = (routes[:, :, None] == expert_ids[None, None, :]).astype(jnp.float32)
    picked = lax.optimization_barrier(jnp.sum(onehot * scores[:, None, :], axis=2))
    mixing = routed_scale * picked / lax.optimization_barrier(jnp.sum(picked, axis=1, keepdims=True))
    expert_mix = lax.optimization_barrier(jnp.sum(onehot * mixing[:, :, None], axis=1))
    chosen = lax.optimization_barrier(jnp.sum(onehot, axis=1)) > 0.5
    capacity = N_EP * MOST

    def one_expert(expert):
        column = chosen[:, expert]
        members = jnp.nonzero(column, size=capacity, fill_value=0)[0].astype(jnp.int32)
        live_count = jnp.sum(column.astype(jnp.int32))
        is_live = jnp.arange(capacity, dtype=jnp.int32) < live_count
        gate_block = lax.dynamic_slice_in_dim(gate_all, expert * HID, HID, 1)
        up_block = lax.dynamic_slice_in_dim(up_all, expert * HID, HID, 1)
        down_block = lax.dynamic_slice_in_dim(down_all, expert * D, D, 1)
        outcome = expert_rows(normed[members], gate_block, up_block, down_block)
        share_weight = jnp.where(is_live, expert_mix[members, expert], 0.0)
        return (members, share_weight[:, None] * outcome.astype(jnp.float32))
    members, contributions = lax.map(one_expert, expert_ids)
    combined = jnp.zeros((TOKENS, D), jnp.float32).at[members.reshape(-1)].add(contributions.reshape(-1, D))
    return (current + combined).astype(jnp.bfloat16)

def reference(inputs, norm_gain, router_weight, gate_weight, up_weight, down_weight, routing):

    def one_batch(batch_index):

        def one_layer(activations, layer_index):
            updated = moe_layer(activations, norm_gain[layer_index], router_weight[layer_index], gate_weight[layer_index], up_weight[layer_index], down_weight[layer_index], routing[layer_index, batch_index])
            return (updated, None)
        finished, unused = lax.scan(one_layer, inputs[batch_index], jnp.arange(LAYERS, dtype=jnp.int32))
        return finished
    return lax.map(one_batch, jnp.arange(MB, dtype=jnp.int32))
```

```python
import functools

import jax
import jax.numpy as jnp
from jax import lax
from jax.experimental import pallas as pl
from jax.experimental.pallas import tpu as pltpu
from jax.sharding import PartitionSpec as P

routed_scale = 2.5
norm_epsilon = 1e-06
most = 5
pieces = 8
half_pieces = 4
back_rows = 24
mib = 1 << 20
bf16 = jnp.bfloat16
f32 = jnp.float32


def call(body, outs, inputs, spaces, scratch=(), vmem=60, flops=0, moved=0):
    kinds = {"v": pltpu.VMEM, "a": pl.ANY}
    return pl.pallas_call(
        body,
        out_shape=outs,
        in_specs=[pl.BlockSpec(memory_space=kinds[k]) for k in spaces],
        out_specs=tuple(pl.BlockSpec(memory_space=pltpu.VMEM) for _ in outs)
        if isinstance(outs, tuple)
        else pl.BlockSpec(memory_space=pltpu.VMEM),
        scratch_shapes=list(scratch),
        compiler_params=pltpu.CompilerParams(vmem_limit_bytes=vmem * mib),
        cost_estimate=pl.CostEstimate(flops=flops, bytes_accessed=moved, transcendentals=0),
    )(*inputs)


def micro_of(step, micros):
    return jnp.clip(step - lax.axis_index("pp"), 0, micros - 1)


def fetch_pieces(inputs, micro, target, sems):
    tokens = inputs.shape[1]
    piece = target.shape[1]
    return [
        pltpu.make_async_copy(
            inputs.at[micro, :, pl.ds(b * piece, piece)],
            target.at[pl.ds(b * tokens, tokens), :],
            sems.at[b],
        )
        for b in range(pieces)
    ]


def normalize(x, gain, target):
    stack, piece = x.shape
    tokens = stack // pieces
    total = jnp.zeros((tokens, 1), f32)
    for b in range(pieces):
        part = x[b * tokens : (b + 1) * tokens, :].astype(f32)
        total = total + jnp.sum(part * part, axis=1, keepdims=True)
    scale = lax.rsqrt(total * (1.0 / (pieces * piece)) + norm_epsilon)
    for b in range(pieces):
        part = slice(b * tokens, (b + 1) * tokens)
        weight = gain[:, b * piece : (b + 1) * piece]
        target[part, :] = (x[part, :].astype(f32) * scale * weight).astype(bf16)


def send_blocks(step, x, gain, targets, blocks, normed, placed):
    normalize(x, gain, normed)
    aims = targets[micro_of(step, targets.shape[0])]
    rows = lax.broadcasted_iota(jnp.int32, placed.shape, 0)
    hit = rows == aims[0:1, :]
    for n in range(1, 4):
        hit = jnp.logical_or(hit, rows == aims[n : n + 1, :])
    placed[...] = hit.astype(f32).astype(bf16)
    blocks[...] = jnp.dot(placed[...], normed[...], preferred_element_type=f32).astype(bf16)


def first_kernel(inputs, gain, targets, blocks, x_out, normed, placed, sems):
    copies = fetch_pieces(inputs, 0, x_out, sems)
    for copy in copies:
        copy.start()
    for copy in copies:
        copy.wait()
    send_blocks(0, x_out, gain, targets, blocks, normed, placed)


def send_kernel(step, x, gain, targets, blocks, normed, placed):
    send_blocks(step, x, gain, targets, blocks, normed, placed)


def mix_kernel(step, x, inputs, gain, router, routing, places, x_out, matrix, normed, sems):
    micros = routing.shape[0]
    experts = router.shape[0]
    tokens = x.shape[0] // pieces
    piece = x.shape[1]
    columns = matrix.shape[1]
    x_out[...] = x[...]
    live = 1.0
    if step < micros - 1:
        last = lax.axis_index("pp") == lax.axis_size("pp") - 1
        live = jnp.where(last, 0.0, 1.0)

        @pl.when(last)
        def _():
            copies = fetch_pieces(inputs, step + 1, x_out, sems)
            for copy in copies:
                copy.start()
            for copy in copies:
                copy.wait()

    normalize(x, gain, normed)
    logits = jnp.zeros((tokens, experts), f32)
    for b in range(pieces):
        logits = logits + lax.dot_general(
            normed[b * tokens : (b + 1) * tokens, :],
            router[:, b * piece : (b + 1) * piece],
            (((1,), (1,)), ((), ())),
            preferred_element_type=f32,
        )
    micro = micro_of(step, micros)
    chosen = routing[micro]
    place = places[micro]
    expert = lax.broadcasted_iota(jnp.int32, (tokens, experts), 1)
    named = jnp.logical_or(expert == chosen[:, 0:1], expert == chosen[:, 1:2])
    scores = jnp.where(named, 1.0 / (1.0 + jnp.exp(-logits)), 0.0)
    mixing = routed_scale * scores / jnp.sum(scores, axis=1, keepdims=True)
    high = mixing.astype(bf16)
    low = (mixing - high.astype(f32)).astype(bf16)

    column = lax.broadcasted_iota(jnp.int32, (1, columns), 1)
    sender = sum((column >= back_rows * n).astype(jnp.int32) for n in range(1, columns // back_rows))
    within = column - sender * back_rows
    owner = sender >> 1
    slot = owner * most + (within >> 2)
    used = within < most * half_pieces
    part_of = (sender & 1) * half_pieces + (within & 3)
    spread = (lax.broadcasted_iota(jnp.int32, (experts, columns), 0) == owner).astype(f32)
    hit = jnp.logical_or(slot == place[:, 0:1], slot == place[:, 1:2])
    hit = jnp.where(jnp.logical_and(hit, used), live, 0.0)
    for n, part in enumerate((high, low)):
        wide = jnp.dot(part, spread.astype(bf16), preferred_element_type=f32) * hit
        for b in range(pieces):
            row = (n * pieces + b) * tokens
            matrix[row : row + tokens, :] = jnp.where(part_of == b, wide, 0.0).astype(bf16)


def hidden_kernel(received, gate, up, hidden, gate_held, up_held, rows, sums, sems):
    piece = received.shape[1]
    group = 256
    total = received.shape[0]
    depth = gate.shape[0]
    chunk = 1024
    starts = list(range(0, total, group))
    sizes = [min(group, total - start) for start in starts]
    weights = []
    for n, start in enumerate(range(0, depth, chunk)):
        part = pl.ds(start, chunk)
        at = 2 * n
        weights.append(
            (
                pltpu.make_async_copy(gate.at[part, :], gate_held.at[part, :], sems.at[at]),
                pltpu.make_async_copy(up.at[part, :], up_held.at[part, :], sems.at[at + 1]),
            )
        )
    for pair in weights:
        for copy in pair:
            copy.start()
    for n, (start, size) in enumerate(zip(starts, sizes)):
        per = size // pieces
        source = lax.broadcasted_iota(jnp.int32, (size, size), 1)
        place = lax.broadcasted_iota(jnp.int32, (size, size), 0)
        target = (source & (pieces - 1)) * per + (source >> 3)
        order = (target == place).astype(f32).astype(bf16)
        moved = jnp.dot(
            order, received[start : start + size, :], preferred_element_type=f32
        ).astype(bf16)
        for q in range(pieces):
            rows[start // pieces : start // pieces + per, q * piece : (q + 1) * piece] = moved[
                q * per : (q + 1) * per
            ]
    for n, start in enumerate(range(0, depth, chunk)):
        part = slice(start, start + chunk)
        for which, held_weight in enumerate((gate_held, up_held)):
            weights[n][which].wait()
            product = jnp.dot(rows[:, part], held_weight[part, :], preferred_element_type=f32)
            if n == 0:
                sums[which] = product
            else:
                sums[which] += product
    gate_proj = sums[0]
    hidden[...] = (gate_proj / (1.0 + jnp.exp(-gate_proj)) * sums[1]).astype(bf16)


def own_kernel(own, down, partial, down_held, sems):
    half = own.shape[1]
    member = lax.axis_index("ep") % 2
    mine = pl.multiple_of(member * half, half)
    theirs = pl.multiple_of((1 - member) * half, half)
    piece = partial.shape[2]
    copies = [
        pltpu.make_async_copy(
            down.at[pl.ds(mine, half), pl.ds(q * piece, piece)],
            down_held.at[pl.ds(0, half), pl.ds(q * piece, piece)],
            sems.at[q],
        )
        for q in range(half_pieces)
    ]
    last = pltpu.make_async_copy(
        down.at[pl.ds(theirs, half), :], down_held.at[pl.ds(half, half), :], sems.at[half_pieces]
    )
    for copy in copies:
        copy.start()
    last.start()
    for q in range(half_pieces):
        copies[q].wait()
        partial[q] = jnp.dot(
            own[...],
            down_held[0:half, q * piece : (q + 1) * piece],
            preferred_element_type=f32,
        )
    last.wait()


def back_kernel(other, down, partial, blocks, stacked):
    count, half = other.shape
    piece = blocks.shape[1]
    for q in range(half_pieces):
        outcome = partial[q] + jnp.dot(
            other[...],
            down[half : 2 * half, q * piece : (q + 1) * piece],
            preferred_element_type=f32,
        )
        stacked[q * count : (q + 1) * count, :] = outcome.astype(bf16)
    shape = (blocks.shape[0], half_pieces * count)
    source = lax.broadcasted_iota(jnp.int32, (1, shape[1]), 1)
    quarter = sum((source >= q * count).astype(jnp.int32) for q in range(1, half_pieces))
    rest = source - quarter * count
    sender = (rest * 205) >> 10
    slot = rest - sender * most
    target = sender * back_rows + slot * half_pieces + quarter
    place = lax.broadcasted_iota(jnp.int32, shape, 0)
    order = (target == place).astype(f32).astype(bf16)
    blocks[...] = jnp.dot(order, stacked[...], preferred_element_type=f32).astype(bf16)


def join_kernel(x, matrix, returned, x_out):
    both = jnp.dot(matrix[...], returned[...], preferred_element_type=f32)
    rows = x.shape[0]
    x_out[...] = (x[...].astype(f32) + (both[0:rows] + both[rows : 2 * rows])).astype(bf16)


def final_kernel(updated, *refs):
    out = refs[-1]
    total = refs[0][...]
    for ref in refs[1:-1]:
        total = total + ref[...]
    last = lax.axis_index("pp") == lax.axis_size("pp") - 1
    total = jnp.where(last, updated[...].astype(f32), total.astype(f32)).astype(bf16)
    tokens = out.shape[0]
    piece = updated.shape[1]
    for b in range(pieces):
        out[:, b * piece : (b + 1) * piece] = total[b * tokens : (b + 1) * tokens]


def slot_places(routing, experts):
    count = routing.shape[0]
    expert_of = routing.reshape(count, -1)
    same = expert_of[:, :, None] == expert_of[:, None, :]
    number = jnp.arange(expert_of.shape[1])
    before = number[None, :] < number[:, None]
    earlier = jnp.sum(jnp.logical_and(same, before[None]).astype(jnp.int32), axis=2)
    return (expert_of * most + earlier).reshape(routing.shape)


def on_device(inputs, norm_gain, router_weight, gate_weight, up_weight, down_weight, routing):
    sections = lax.axis_size("pp")
    devices = lax.axis_size("ep")
    micros, tokens, width = inputs.shape
    experts = router_weight.shape[2]
    piece = width // pieces
    rows = devices * most
    half = gate_weight.shape[2]
    stack = pieces * tokens
    shape = jax.ShapeDtypeStruct
    vmem = pltpu.VMEM
    dma = pltpu.SemaphoreType.DMA

    routes = routing[0]
    places = slot_places(routes, experts)
    owner, slot = places // most, places % most
    choice = jnp.swapaxes(owner * (2 * most) + slot, 1, 2)
    aims = jnp.concatenate([choice, choice + most], axis=1)
    aims = aims[:, :, None, :] * pieces + jnp.arange(pieces)[None, None, :, None]
    aims = aims.reshape(micros, 4, stack).astype(jnp.int32)
    router = router_weight[0].T
    gate, up, down = gate_weight[0], up_weight[0], down_weight[0]

    hops = [(s, (s + 1) % sections) for s in range(sections)]
    partners = [(i, i ^ 1) for i in range(devices)]
    block_shape = shape((rows * pieces, piece), bf16)
    stack_scratch = vmem((stack, piece), bf16)
    place_scratch = vmem((rows * pieces, stack), bf16)
    done = []
    for step in range(sections + micros - 1):
        if step == 0:
            blocks, carried = call(
                first_kernel,
                (block_shape, shape((stack, piece), bf16)),
                (inputs, norm_gain, aims),
                "avv",
                scratch=(stack_scratch, place_scratch, dma((pieces,))),
                vmem=16,
                flops=2 * 640 * 128 * piece,
                moved=2 * mib,
            )
        else:
            blocks = call(
                functools.partial(send_kernel, step),
                block_shape,
                (carried, norm_gain, aims),
                "vvv",
                scratch=(stack_scratch, place_scratch),
                vmem=16,
                flops=2 * 640 * 128 * piece,
                moved=2 * mib,
            )
        received = lax.all_to_all(blocks, "ep", split_axis=0, concat_axis=0, tiled=True)
        x, matrix = call(
            functools.partial(mix_kernel, step),
            (
                vmem((stack, piece), bf16),
                vmem((2 * stack, devices * back_rows), bf16),
            ),
            (carried, inputs, norm_gain, router, routes, places),
            "vavvvv",
            scratch=(stack_scratch, dma((pieces,))),
            vmem=60,
            flops=2 * tokens * width * 128,
            moved=4 * mib,
        )
        hidden = call(
            hidden_kernel,
            shape((rows, half), bf16),
            (received, gate, up),
            "vaa",
            scratch=(
                vmem((width, half), bf16),
                vmem((width, half), bf16),
                vmem((rows, width), bf16),
                vmem((2, rows, half), f32),
                dma((14,)),
            ),
            vmem=57,
            flops=4 * rows * width * half,
            moved=15 * mib,
        )
        partner = lax.ppermute(hidden, "ep", partners)
        partial, down_held = call(
            own_kernel,
            (vmem((half_pieces, rows, piece), f32), vmem(down.shape, bf16)),
            (hidden, down),
            "va",
            scratch=(dma((half_pieces + 1,)),),
            vmem=48,
            flops=2 * rows * half * width // 2,
            moved=8 * mib,
        )
        back = call(
            back_kernel,
            shape((devices * back_rows, piece), bf16),
            (partner, down_held, partial),
            "vvv",
            scratch=(vmem((half_pieces * rows, piece), bf16),),
            vmem=16,
            flops=2 * rows * half * width // 2,
            moved=4 * mib,
        )
        returned = lax.all_to_all(back, "ep", split_axis=0, concat_axis=0, tiled=True)
        updated = call(
            join_kernel,
            shape((stack, piece), bf16),
            (x, matrix, returned),
            "vvv",
            vmem=16,
            flops=2 * 256 * 384 * piece,
            moved=2 * mib,
        )
        target = step - (sections - 1)
        if 0 <= target < micros - 1:
            done.append(lax.ppermute(updated, "pp", [(sections - 1, target)]))
        if step < sections + micros - 2:
            carried = lax.ppermute(updated, "pp", hops)
    final = call(
        final_kernel,
        shape((tokens, width), bf16),
        (updated, *done),
        "v" * (1 + len(done)),
        vmem=16,
        moved=3 * mib,
    )
    return final[None]


def solution(mesh):
    return jax.shard_map(
        on_device,
        mesh=mesh,
        in_specs=(
            P(None, "ep", None),
            P("pp", None),
            P("pp", None, None),
            P("pp", None, "ep"),
            P("pp", None, "ep"),
            P("pp", None, "ep"),
            P("pp", None, "ep", None),
        ),
        out_specs=P("pp", "ep", None),
        check_vma=False,
    )
```

```python
import functools

import jax
import jax.numpy as jnp
from jax import lax
from jax.experimental import pallas as pl
from jax.experimental.pallas import tpu as pltpu
from jax.sharding import PartitionSpec as P

routed_scale = 2.5
norm_epsilon = 1e-06
most = 5
pieces = 8
half_pieces = 4
back_rows = 24
mib = 1 << 20
bf16 = jnp.bfloat16
f32 = jnp.float32


def weight_chunks(depth):
    chunks = []
    start = 0
    while start < depth:
        size = min(1024 if depth - start > 1536 else 512, depth - start)
        chunks.append((start, size))
        start += size
    return chunks


def call(body, outs, inputs, spaces, scratch=(), vmem=60, flops=0, moved=0):
    kinds = {"v": pltpu.VMEM, "a": pl.ANY}
    return pl.pallas_call(
        body,
        out_shape=outs,
        in_specs=[pl.BlockSpec(memory_space=kinds[k]) for k in spaces],
        out_specs=tuple(pl.BlockSpec(memory_space=pltpu.VMEM) for _ in outs)
        if isinstance(outs, tuple)
        else pl.BlockSpec(memory_space=pltpu.VMEM),
        scratch_shapes=list(scratch),
        compiler_params=pltpu.CompilerParams(vmem_limit_bytes=vmem * mib),
        cost_estimate=pl.CostEstimate(flops=flops, bytes_accessed=moved, transcendentals=0),
    )(*inputs)


def micro_of(step, micros):
    return jnp.clip(step - lax.axis_index("pp"), 0, micros - 1)


def fetch_pieces(inputs, micro, target, sems):
    tokens = inputs.shape[1]
    piece = target.shape[1]
    return [
        pltpu.make_async_copy(
            inputs.at[micro, :, pl.ds(b * piece, piece)],
            target.at[pl.ds(b * tokens, tokens), :],
            sems.at[b],
        )
        for b in range(pieces)
    ]


def normalize(x, gain, target):
    stack, piece = x.shape
    tokens = stack // pieces
    total = jnp.zeros((tokens, 1), f32)
    for b in range(pieces):
        part = x[b * tokens : (b + 1) * tokens, :].astype(f32)
        total = total + jnp.sum(part * part, axis=1, keepdims=True)
    scale = lax.rsqrt(total * (1.0 / (pieces * piece)) + norm_epsilon)
    for b in range(pieces):
        part = slice(b * tokens, (b + 1) * tokens)
        weight = gain[:, b * piece : (b + 1) * piece]
        target[part, :] = (x[part, :].astype(f32) * scale * weight).astype(bf16)


def send_blocks(step, x, gain, targets, blocks, normed, placed):
    normalize(x, gain, normed)
    aims = targets[micro_of(step, targets.shape[0])]
    rows = lax.broadcasted_iota(jnp.int32, placed.shape, 0)
    hit = rows == aims[0:1, :]
    for n in range(1, 4):
        hit = jnp.logical_or(hit, rows == aims[n : n + 1, :])
    placed[...] = hit.astype(f32).astype(bf16)
    blocks[...] = jnp.dot(placed[...], normed[...], preferred_element_type=f32).astype(bf16)


def first_kernel(inputs, gain, targets, blocks, x_out, normed, placed, sems):
    copies = fetch_pieces(inputs, 0, x_out, sems)
    for copy in copies:
        copy.start()
    for copy in copies:
        copy.wait()
    send_blocks(0, x_out, gain, targets, blocks, normed, placed)


def send_kernel(step, x, gain, targets, blocks, normed, placed):
    send_blocks(step, x, gain, targets, blocks, normed, placed)


def mix_kernel(step, x, inputs, gain, router, routing, places, x_out, matrix, normed, sems):
    micros = routing.shape[0]
    experts = router.shape[0]
    tokens = x.shape[0] // pieces
    piece = x.shape[1]
    columns = matrix.shape[1]
    x_out[...] = x[...]
    live = 1.0
    if step < micros - 1:
        last = lax.axis_index("pp") == lax.axis_size("pp") - 1
        live = jnp.where(last, 0.0, 1.0)

        @pl.when(last)
        def _():
            copies = fetch_pieces(inputs, step + 1, x_out, sems)
            for copy in copies:
                copy.start()
            for copy in copies:
                copy.wait()

    normalize(x, gain, normed)
    logits = jnp.zeros((tokens, experts), f32)
    for b in range(pieces):
        logits = logits + lax.dot_general(
            normed[b * tokens : (b + 1) * tokens, :],
            router[:, b * piece : (b + 1) * piece],
            (((1,), (1,)), ((), ())),
            preferred_element_type=f32,
        )
    micro = micro_of(step, micros)
    chosen = routing[micro]
    place = places[micro]
    expert = lax.broadcasted_iota(jnp.int32, (tokens, experts), 1)
    named = jnp.logical_or(expert == chosen[:, 0:1], expert == chosen[:, 1:2])
    scores = jnp.where(named, 1.0 / (1.0 + jnp.exp(-logits)), 0.0)
    mixing = routed_scale * scores / jnp.sum(scores, axis=1, keepdims=True)
    high = mixing.astype(bf16)
    low = (mixing - high.astype(f32)).astype(bf16)

    column = lax.broadcasted_iota(jnp.int32, (1, columns), 1)
    sender = sum((column >= back_rows * n).astype(jnp.int32) for n in range(1, columns // back_rows))
    within = column - sender * back_rows
    owner = sender >> 1
    slot = owner * most + (within >> 2)
    used = within < most * half_pieces
    part_of = (sender & 1) * half_pieces + (within & 3)
    spread = (lax.broadcasted_iota(jnp.int32, (experts, columns), 0) == owner).astype(f32)
    hit = jnp.logical_or(slot == place[:, 0:1], slot == place[:, 1:2])
    hit = jnp.where(jnp.logical_and(hit, used), live, 0.0)
    for n, part in enumerate((high, low)):
        wide = jnp.dot(part, spread.astype(bf16), preferred_element_type=f32) * hit
        for b in range(pieces):
            row = (n * pieces + b) * tokens
            matrix[row : row + tokens, :] = jnp.where(part_of == b, wide, 0.0).astype(bf16)


def hidden_kernel(
    received, gate, up, hidden, held, gate_held, up_held, rows, sums, sems
):
    piece = received.shape[1]
    group = 256
    total = received.shape[0]
    depth = gate.shape[0]
    starts = list(range(0, total, group))
    sizes = [min(group, total - start) for start in starts]
    loads = [
        pltpu.make_async_copy(
            received.at[pl.ds(start, size), :], held.at[pl.ds(start, size), :], sems.at[n]
        )
        for n, (start, size) in enumerate(zip(starts, sizes))
    ]
    chunks = weight_chunks(depth)
    weights = []
    for n, (start, size) in enumerate(chunks):
        part = pl.ds(start, size)
        at = len(starts) + 2 * n
        weights.append(
            (
                pltpu.make_async_copy(gate.at[part, :], gate_held.at[part, :], sems.at[at]),
                pltpu.make_async_copy(up.at[part, :], up_held.at[part, :], sems.at[at + 1]),
            )
        )
    for copy in loads:
        copy.start()
    for pair in weights:
        for copy in pair:
            copy.start()
    for n, (start, size) in enumerate(zip(starts, sizes)):
        per = size // pieces
        source = lax.broadcasted_iota(jnp.int32, (size, size), 1)
        place = lax.broadcasted_iota(jnp.int32, (size, size), 0)
        target = (source & (pieces - 1)) * per + (source >> 3)
        order = (target == place).astype(f32).astype(bf16)
        loads[n].wait()
        moved = jnp.dot(
            order, held[start : start + size, :], preferred_element_type=f32
        ).astype(bf16)
        for q in range(pieces):
            rows[start // pieces : start // pieces + per, q * piece : (q + 1) * piece] = moved[
                q * per : (q + 1) * per
            ]
    for n, (start, size) in enumerate(chunks):
        part = slice(start, start + size)
        for which, held_weight in enumerate((gate_held, up_held)):
            weights[n][which].wait()
            product = jnp.dot(
                rows[:, part], held_weight[part, :], preferred_element_type=f32
            )
            if n == 0:
                sums[which] = product
            else:
                sums[which] += product
    gate_proj = sums[0]
    hidden[...] = (gate_proj / (1.0 + jnp.exp(-gate_proj)) * sums[1]).astype(bf16)


def own_kernel(own, down, partial, down_held, order, sems):
    half = own.shape[1]
    member = lax.axis_index("ep") % 2
    mine = pl.multiple_of(member * half, half)
    theirs = pl.multiple_of((1 - member) * half, half)
    piece = partial.shape[2]
    copies = [
        pltpu.make_async_copy(
            down.at[pl.ds(mine, half), pl.ds(q * piece, piece)],
            down_held.at[pl.ds(0, half), pl.ds(q * piece, piece)],
            sems.at[q],
        )
        for q in range(half_pieces)
    ]
    last = pltpu.make_async_copy(
        down.at[pl.ds(theirs, half), :], down_held.at[pl.ds(half, half), :], sems.at[half_pieces]
    )
    for copy in copies:
        copy.start()
    last.start()
    count = own.shape[0]
    shape = order.shape
    source = lax.broadcasted_iota(jnp.int32, (1, shape[1]), 1)
    quarter = sum((source >= q * count).astype(jnp.int32) for q in range(1, half_pieces))
    rest = source - quarter * count
    sender = (rest * 205) >> 10
    slot = rest - sender * most
    target = sender * back_rows + slot * half_pieces + quarter
    place = lax.broadcasted_iota(jnp.int32, shape, 0)
    order[...] = (target == place).astype(f32).astype(bf16)
    for q in range(half_pieces):
        copies[q].wait()
        partial[q] = jnp.dot(
            own[...],
            down_held[0:half, q * piece : (q + 1) * piece],
            preferred_element_type=f32,
        )
    last.wait()


def back_kernel(other, down, partial, order, blocks, stacked):
    count, half = other.shape
    piece = blocks.shape[1]
    for q in range(half_pieces):
        outcome = partial[q] + jnp.dot(
            other[...],
            down[half : 2 * half, q * piece : (q + 1) * piece],
            preferred_element_type=f32,
        )
        stacked[q * count : (q + 1) * count, :] = outcome.astype(bf16)
    blocks[...] = jnp.dot(order[...], stacked[...], preferred_element_type=f32).astype(bf16)


def join_kernel(x, matrix, returned, x_out):
    both = jnp.dot(matrix[...], returned[...], preferred_element_type=f32)
    rows = x.shape[0]
    x_out[...] = (x[...].astype(f32) + (both[0:rows] + both[rows : 2 * rows])).astype(bf16)


def final_kernel(updated, *refs):
    out = refs[-1]
    total = refs[0][...]
    for ref in refs[1:-1]:
        total = total + ref[...]
    last = lax.axis_index("pp") == lax.axis_size("pp") - 1
    total = jnp.where(last, updated[...].astype(f32), total.astype(f32)).astype(bf16)
    tokens = out.shape[0]
    piece = updated.shape[1]
    for b in range(pieces):
        out[:, b * piece : (b + 1) * piece] = total[b * tokens : (b + 1) * tokens]


def slot_places(routing, experts):
    count = routing.shape[0]
    expert_of = routing.reshape(count, -1)
    same = expert_of[:, :, None] == expert_of[:, None, :]
    number = jnp.arange(expert_of.shape[1])
    before = number[None, :] < number[:, None]
    earlier = jnp.sum(jnp.logical_and(same, before[None]).astype(jnp.int32), axis=2)
    return (expert_of * most + earlier).reshape(routing.shape)


def on_device(inputs, norm_gain, router_weight, gate_weight, up_weight, down_weight, routing):
    sections = lax.axis_size("pp")
    devices = lax.axis_size("ep")
    micros, tokens, width = inputs.shape
    experts = router_weight.shape[2]
    piece = width // pieces
    rows = devices * most
    half = gate_weight.shape[2]
    stack = pieces * tokens
    shape = jax.ShapeDtypeStruct
    vmem = pltpu.VMEM
    dma = pltpu.SemaphoreType.DMA

    routes = routing[0]
    places = slot_places(routes, experts)
    owner, slot = places // most, places % most
    choice = jnp.swapaxes(owner * (2 * most) + slot, 1, 2)
    aims = jnp.concatenate([choice, choice + most], axis=1)
    aims = aims[:, :, None, :] * pieces + jnp.arange(pieces)[None, None, :, None]
    aims = aims.reshape(micros, 4, stack).astype(jnp.int32)
    router = router_weight[0].T
    gate, up, down = gate_weight[0], up_weight[0], down_weight[0]

    hops = [(s, (s + 1) % sections) for s in range(sections)]
    partners = [(i, i ^ 1) for i in range(devices)]
    block_shape = shape((rows * pieces, piece), bf16)
    stack_scratch = vmem((stack, piece), bf16)
    place_scratch = vmem((rows * pieces, stack), bf16)
    done = []
    for step in range(sections + micros - 1):
        if step == 0:
            blocks, carried = call(
                first_kernel,
                (block_shape, shape((stack, piece), bf16)),
                (inputs, norm_gain, aims),
                "avv",
                scratch=(stack_scratch, place_scratch, dma((pieces,))),
                vmem=60,
                flops=2 * 640 * 128 * piece,
                moved=2 * mib,
            )
        else:
            blocks = call(
                functools.partial(send_kernel, step),
                block_shape,
                (carried, norm_gain, aims),
                "vvv",
                scratch=(stack_scratch, place_scratch),
                vmem=16,
                flops=2 * 640 * 128 * piece,
                moved=2 * mib,
            )
        received = lax.all_to_all(blocks, "ep", split_axis=0, concat_axis=0, tiled=True)
        x, matrix = call(
            functools.partial(mix_kernel, step),
            (
                vmem((stack, piece), bf16),
                vmem((2 * stack, devices * back_rows), bf16),
            ),
            (carried, inputs, norm_gain, router, routes, places),
            "vavvvv",
            scratch=(stack_scratch, dma((pieces,))),
            vmem=60,
            flops=2 * tokens * width * 128,
            moved=4 * mib,
        )
        hidden = call(
            hidden_kernel,
            shape((rows, half), bf16),
            (received, gate, up),
            "aaa",
            scratch=(
                vmem((rows * pieces, piece), bf16),
                vmem((width, half), bf16),
                vmem((width, half), bf16),
                vmem((rows, width), bf16),
                vmem((2, rows, half), f32),
                dma((3 + 2 * len(weight_chunks(width)),)),
            ),
            vmem=57,
            flops=4 * rows * width * half,
            moved=15 * mib,
        )
        partner = lax.ppermute(hidden, "ep", partners)
        partial, down_held, order = call(
            own_kernel,
            (
                vmem((half_pieces, rows, piece), f32),
                vmem(down.shape, bf16),
                vmem((devices * back_rows, half_pieces * rows), bf16),
            ),
            (hidden, down),
            "va",
            scratch=(dma((half_pieces + 1,)),),
            vmem=48,
            flops=2 * rows * half * width // 2,
            moved=8 * mib,
        )
        back = call(
            back_kernel,
            shape((devices * back_rows, piece), bf16),
            (partner, down_held, partial, order),
            "vvvv",
            scratch=(vmem((half_pieces * rows, piece), bf16),),
            vmem=16,
            flops=2 * rows * half * width // 2,
            moved=4 * mib,
        )
        returned = lax.all_to_all(back, "ep", split_axis=0, concat_axis=0, tiled=True)
        updated = call(
            join_kernel,
            shape((stack, piece), bf16),
            (x, matrix, returned),
            "vvv",
            vmem=16,
            flops=2 * 256 * 384 * piece,
            moved=2 * mib,
        )
        target = step - (sections - 1)
        if 0 <= target < micros - 1:
            done.append(lax.ppermute(updated, "pp", [(sections - 1, target)]))
        if step < sections + micros - 2:
            carried = lax.ppermute(updated, "pp", hops)
    final = call(
        final_kernel,
        shape((tokens, width), bf16),
        (updated, *done),
        "v" * (1 + len(done)),
        vmem=16,
        moved=3 * mib,
    )
    return final[None]


def solution(mesh):
    return jax.shard_map(
        on_device,
        mesh=mesh,
        in_specs=(
            P(None, "ep", None),
            P("pp", None),
            P("pp", None, None),
            P("pp", None, "ep"),
            P("pp", None, "ep"),
            P("pp", None, "ep"),
            P("pp", None, "ep", None),
        ),
        out_specs=P("pp", "ep", None),
        check_vma=False,
    )
```

```python
import functools

import jax
import jax.numpy as jnp
from jax import lax
from jax.experimental import pallas as pl
from jax.experimental.pallas import tpu as pltpu
from jax.sharding import PartitionSpec as P

routed_scale = 2.5
norm_epsilon = 1e-06
most = 5
pieces = 8
half_pieces = 4
back_rows = 24
mib = 1 << 20
bf16 = jnp.bfloat16
f32 = jnp.float32


def weight_chunks(depth):
    chunks = []
    start = 0
    while start < depth:
        size = min(1024 if depth - start > 1536 else 512, depth - start)
        chunks.append((start, size))
        start += size
    return chunks


def call(body, outs, inputs, spaces, scratch=(), vmem=60, flops=0, moved=0):
    kinds = {"v": pltpu.VMEM, "a": pl.ANY}
    return pl.pallas_call(
        body,
        out_shape=outs,
        in_specs=[pl.BlockSpec(memory_space=kinds[k]) for k in spaces],
        out_specs=tuple(pl.BlockSpec(memory_space=pltpu.VMEM) for _ in outs)
        if isinstance(outs, tuple)
        else pl.BlockSpec(memory_space=pltpu.VMEM),
        scratch_shapes=list(scratch),
        compiler_params=pltpu.CompilerParams(vmem_limit_bytes=vmem * mib),
        cost_estimate=pl.CostEstimate(flops=flops, bytes_accessed=moved, transcendentals=0),
    )(*inputs)


def micro_of(step, micros):
    return jnp.clip(step - lax.axis_index("pp"), 0, micros - 1)


def fetch_pieces(inputs, micro, target, sems):
    tokens = inputs.shape[1]
    piece = target.shape[1]
    return [
        pltpu.make_async_copy(
            inputs.at[micro, :, pl.ds(b * piece, piece)],
            target.at[pl.ds(b * tokens, tokens), :],
            sems.at[b],
        )
        for b in range(pieces)
    ]


def normalize(x, gain, target):
    stack, piece = x.shape
    tokens = stack // pieces
    total = jnp.zeros((tokens, 1), f32)
    for b in range(pieces):
        part = x[b * tokens : (b + 1) * tokens, :].astype(f32)
        total = total + jnp.sum(part * part, axis=1, keepdims=True)
    scale = lax.rsqrt(total * (1.0 / (pieces * piece)) + norm_epsilon)
    for b in range(pieces):
        part = slice(b * tokens, (b + 1) * tokens)
        weight = gain[:, b * piece : (b + 1) * piece]
        target[part, :] = (x[part, :].astype(f32) * scale * weight).astype(bf16)


def send_blocks(step, x, gain, targets, blocks, normed, placed):
    normalize(x, gain, normed)
    aims = targets[micro_of(step, targets.shape[0])]
    rows = lax.broadcasted_iota(jnp.int32, placed.shape, 0)
    hit = rows == aims[0:1, :]
    for n in range(1, 4):
        hit = jnp.logical_or(hit, rows == aims[n : n + 1, :])
    placed[...] = hit.astype(f32).astype(bf16)
    blocks[...] = jnp.dot(placed[...], normed[...], preferred_element_type=f32).astype(bf16)


def first_kernel(inputs, gain, targets, blocks, x_out, normed, placed, sems):
    copies = fetch_pieces(inputs, 0, x_out, sems)
    for copy in copies:
        copy.start()
    for copy in copies:
        copy.wait()
    send_blocks(0, x_out, gain, targets, blocks, normed, placed)


def send_kernel(step, x, gain, targets, blocks, normed, placed):
    send_blocks(step, x, gain, targets, blocks, normed, placed)


def mix_kernel(step, x, inputs, gain, router, routing, places, x_out, matrix, normed, sems):
    micros = routing.shape[0]
    experts = router.shape[0]
    tokens = x.shape[0] // pieces
    piece = x.shape[1]
    columns = matrix.shape[1]
    x_out[...] = x[...]
    live = step - lax.axis_index("pp") < micros
    if step < micros - 1:
        last = lax.axis_index("pp") == lax.axis_size("pp") - 1
        live = jnp.logical_not(last)

        @pl.when(last)
        def _():
            copies = fetch_pieces(inputs, step + 1, x_out, sems)
            for copy in copies:
                copy.start()
            for copy in copies:
                copy.wait()

    normalize(x, gain, normed)
    logits = jnp.zeros((tokens, experts), f32)
    for b in range(pieces):
        logits = logits + lax.dot_general(
            normed[b * tokens : (b + 1) * tokens, :],
            router[:, b * piece : (b + 1) * piece],
            (((1,), (1,)), ((), ())),
            preferred_element_type=f32,
        )
    micro = micro_of(step, micros)
    chosen = routing[micro]
    place = places[micro]
    expert = lax.broadcasted_iota(jnp.int32, (tokens, experts), 1)
    named = jnp.logical_or(expert == chosen[:, 0:1], expert == chosen[:, 1:2])
    scores = jnp.where(named, 1.0 / (1.0 + jnp.exp(-logits)), 0.0)
    mixing = routed_scale * scores / jnp.sum(scores, axis=1, keepdims=True)
    high = mixing.astype(bf16)
    low = (mixing - high.astype(f32)).astype(bf16)

    column = lax.broadcasted_iota(jnp.int32, (1, columns), 1)
    sender = sum((column >= back_rows * n).astype(jnp.int32) for n in range(1, columns // back_rows))
    within = column - sender * back_rows
    owner = sender >> 1
    slot = owner * most + (within >> 2)
    micro_slot = jnp.where(live, slot, -1)
    used = within < most * half_pieces
    part_of = (sender & 1) * half_pieces + (within & 3)
    spread = (lax.broadcasted_iota(jnp.int32, (experts, columns), 0) == owner).astype(f32)
    hit = jnp.logical_or(slot == place[:, 0:1], slot == place[:, 1:2])
    hit = jnp.logical_and(jnp.logical_and(hit, used), micro_slot >= 0)
    for n, part in enumerate((high, low)):
        wide = jnp.dot(part, spread.astype(bf16), preferred_element_type=f32)
        wide = jnp.where(hit, wide, 0.0)
        for b in range(pieces):
            row = (n * pieces + b) * tokens
            matrix[row : row + tokens, :] = jnp.where(part_of == b, wide, 0.0).astype(bf16)


def hidden_kernel(
    received, gate, up, hidden, held, gate_held, up_held, rows, sums, sems
):
    piece = received.shape[1]
    group = 256
    total = received.shape[0]
    depth = gate.shape[0]
    starts = list(range(0, total, group))
    sizes = [min(group, total - start) for start in starts]
    loads = [
        pltpu.make_async_copy(
            received.at[pl.ds(start, size), :], held.at[pl.ds(start, size), :], sems.at[n]
        )
        for n, (start, size) in enumerate(zip(starts, sizes))
    ]
    chunks = weight_chunks(depth)
    weights = []
    for n, (start, size) in enumerate(chunks):
        part = pl.ds(start, size)
        at = len(starts) + 2 * n
        weights.append(
            (
                pltpu.make_async_copy(gate.at[part, :], gate_held.at[part, :], sems.at[at]),
                pltpu.make_async_copy(up.at[part, :], up_held.at[part, :], sems.at[at + 1]),
            )
        )
    for copy in loads:
        copy.start()
    for pair in weights:
        for copy in pair:
            copy.start()
    for n, (start, size) in enumerate(zip(starts, sizes)):
        per = size // pieces
        source = lax.broadcasted_iota(jnp.int32, (size, size), 1)
        place = lax.broadcasted_iota(jnp.int32, (size, size), 0)
        target = (source & (pieces - 1)) * per + (source >> 3)
        order = (target == place).astype(f32).astype(bf16)
        loads[n].wait()
        moved = jnp.dot(
            order, held[start : start + size, :], preferred_element_type=f32
        ).astype(bf16)
        for q in range(pieces):
            rows[start // pieces : start // pieces + per, q * piece : (q + 1) * piece] = moved[
                q * per : (q + 1) * per
            ]
    for n, (start, size) in enumerate(chunks):
        part = slice(start, start + size)
        for which, held_weight in enumerate((gate_held, up_held)):
            weights[n][which].wait()
            product = jnp.dot(
                rows[:, part], held_weight[part, :], preferred_element_type=f32
            )
            if n == 0:
                sums[which] = product
            else:
                sums[which] += product
    gate_proj = sums[0]
    hidden[...] = (gate_proj / (1.0 + jnp.exp(-gate_proj)) * sums[1]).astype(bf16)


def own_kernel(own, down, partial, down_held, order, sems):
    half = own.shape[1]
    member = lax.axis_index("ep") % 2
    mine = pl.multiple_of(member * half, half)
    theirs = pl.multiple_of((1 - member) * half, half)
    piece = partial.shape[2]
    copies = [
        pltpu.make_async_copy(
            down.at[pl.ds(mine, half), pl.ds(q * piece, piece)],
            down_held.at[pl.ds(0, half), pl.ds(q * piece, piece)],
            sems.at[q],
        )
        for q in range(half_pieces)
    ]
    last = pltpu.make_async_copy(
        down.at[pl.ds(theirs, half), :], down_held.at[pl.ds(half, half), :], sems.at[half_pieces]
    )
    for copy in copies:
        copy.start()
    last.start()
    count = own.shape[0]
    shape = order.shape
    source = lax.broadcasted_iota(jnp.int32, (1, shape[1]), 1)
    quarter = sum((source >= q * count).astype(jnp.int32) for q in range(1, half_pieces))
    rest = source - quarter * count
    sender = (rest * 205) >> 10
    slot = rest - sender * most
    target = sender * back_rows + slot * half_pieces + quarter
    place = lax.broadcasted_iota(jnp.int32, shape, 0)
    order[...] = (target == place).astype(f32).astype(bf16)
    for q in range(half_pieces):
        copies[q].wait()
        partial[q] = jnp.dot(
            own[...],
            down_held[0:half, q * piece : (q + 1) * piece],
            preferred_element_type=f32,
        )
    last.wait()


def back_kernel(other, down, partial, order, blocks, stacked):
    count, half = other.shape
    piece = blocks.shape[1]
    for q in range(half_pieces):
        outcome = partial[q] + jnp.dot(
            other[...],
            down[half : 2 * half, q * piece : (q + 1) * piece],
            preferred_element_type=f32,
        )
        stacked[q * count : (q + 1) * count, :] = outcome.astype(bf16)
    blocks[...] = jnp.dot(order[...], stacked[...], preferred_element_type=f32).astype(bf16)


def join_kernel(x, matrix, returned, x_out):
    both = jnp.dot(matrix[...], returned[...], preferred_element_type=f32)
    rows = x.shape[0]
    x_out[...] = (x[...].astype(f32) + (both[0:rows] + both[rows : 2 * rows])).astype(bf16)


def final_kernel(*refs):
    out = refs[-1]
    section = lax.axis_index("pp")
    tokens = out.shape[0]
    piece = refs[0].shape[1]
    for n, ref in enumerate(refs[:-1]):

        @pl.when(section == n)
        def _():
            for b in range(pieces):
                out[:, b * piece : (b + 1) * piece] = ref[b * tokens : (b + 1) * tokens, :]


def slot_places(routing, experts):
    count = routing.shape[0]
    expert_of = routing.reshape(count, -1)
    same = expert_of[:, :, None] == expert_of[:, None, :]
    number = jnp.arange(expert_of.shape[1])
    before = number[None, :] < number[:, None]
    earlier = jnp.sum(jnp.logical_and(same, before[None]).astype(jnp.int32), axis=2)
    return (expert_of * most + earlier).reshape(routing.shape)


def on_device(inputs, norm_gain, router_weight, gate_weight, up_weight, down_weight, routing):
    sections = lax.axis_size("pp")
    devices = lax.axis_size("ep")
    micros, tokens, width = inputs.shape
    experts = router_weight.shape[2]
    piece = width // pieces
    rows = devices * most
    half = gate_weight.shape[2]
    stack = pieces * tokens
    shape = jax.ShapeDtypeStruct
    vmem = pltpu.VMEM
    dma = pltpu.SemaphoreType.DMA

    routes = routing[0]
    places = slot_places(routes, experts)
    owner, slot = places // most, places % most
    choice = jnp.swapaxes(owner * (2 * most) + slot, 1, 2)
    aims = jnp.concatenate([choice, choice + most], axis=1)
    aims = aims[:, :, None, :] * pieces + jnp.arange(pieces)[None, None, :, None]
    aims = aims.reshape(micros, 4, stack).astype(jnp.int32)
    router = router_weight[0].T
    gate, up, down = gate_weight[0], up_weight[0], down_weight[0]

    hops = [(s, (s + 1) % sections) for s in range(sections)]
    partners = [(i, i ^ 1) for i in range(devices)]
    block_shape = shape((rows * pieces, piece), bf16)
    stack_scratch = vmem((stack, piece), bf16)
    place_scratch = vmem((rows * pieces, stack), bf16)
    kept = [None] * micros
    ring = micros // 2
    for step in range(sections + micros - 1):
        if step == 0:
            blocks, carried = call(
                first_kernel,
                (block_shape, shape((stack, piece), bf16)),
                (inputs, norm_gain, aims),
                "avv",
                scratch=(stack_scratch, place_scratch, dma((pieces,))),
                vmem=60,
                flops=2 * 640 * 128 * piece,
                moved=2 * mib,
            )
        else:
            blocks = call(
                functools.partial(send_kernel, step),
                block_shape,
                (carried, norm_gain, aims),
                "vvv",
                scratch=(stack_scratch, place_scratch),
                vmem=16,
                flops=2 * 640 * 128 * piece,
                moved=2 * mib,
            )
        received = lax.all_to_all(blocks, "ep", split_axis=0, concat_axis=0, tiled=True)
        x, matrix = call(
            functools.partial(mix_kernel, step),
            (
                vmem((stack, piece), bf16),
                vmem((2 * stack, devices * back_rows), bf16),
            ),
            (carried, inputs, norm_gain, router, routes, places),
            "vavvvv",
            scratch=(stack_scratch, dma((pieces,))),
            vmem=60,
            flops=2 * tokens * width * 128,
            moved=4 * mib,
        )
        hidden = call(
            hidden_kernel,
            shape((rows, half), bf16),
            (received, gate, up),
            "aaa",
            scratch=(
                vmem((rows * pieces, piece), bf16),
                vmem((width, half), bf16),
                vmem((width, half), bf16),
                vmem((rows, width), bf16),
                vmem((2, rows, half), f32),
                dma((3 + 2 * len(weight_chunks(width)),)),
            ),
            vmem=57,
            flops=4 * rows * width * half,
            moved=15 * mib,
        )
        partner = lax.ppermute(hidden, "ep", partners)
        partial, down_held, order = call(
            own_kernel,
            (
                vmem((half_pieces, rows, piece), f32),
                vmem(down.shape, bf16),
                vmem((devices * back_rows, half_pieces * rows), bf16),
            ),
            (hidden, down),
            "va",
            scratch=(dma((half_pieces + 1,)),),
            vmem=48,
            flops=2 * rows * half * width // 2,
            moved=8 * mib,
        )
        back = call(
            back_kernel,
            shape((devices * back_rows, piece), bf16),
            (partner, down_held, partial, order),
            "vvvv",
            scratch=(vmem((half_pieces * rows, piece), bf16),),
            vmem=16,
            flops=2 * rows * half * width // 2,
            moved=4 * mib,
        )
        returned = lax.all_to_all(back, "ep", split_axis=0, concat_axis=0, tiled=True)
        updated = call(
            join_kernel,
            shape((stack, piece), bf16),
            (x, matrix, returned),
            "vvv",
            vmem=16,
            flops=2 * 256 * 384 * piece,
            moved=2 * mib,
        )
        target = step - (sections - 1)
        if ring <= target < micros - 1:
            kept[target] = lax.ppermute(updated, "pp", [(sections - 1, target)])
        if step < sections + micros - 2:
            carried = lax.ppermute(updated, "pp", hops)
            after = step + 1 - sections
            if after >= 0 and after % 2 == 0 and after // 2 < ring:
                kept[after // 2] = carried
    final = call(
        final_kernel,
        shape((tokens, width), bf16),
        (*kept[:-1], updated),
        "v" * micros,
        vmem=16,
        moved=3 * mib,
    )
    return final[None]


def solution(mesh):
    return jax.shard_map(
        on_device,
        mesh=mesh,
        in_specs=(
            P(None, "ep", None),
            P("pp", None),
            P("pp", None, None),
            P("pp", None, "ep"),
            P("pp", None, "ep"),
            P("pp", None, "ep"),
            P("pp", None, "ep", None),
        ),
        out_specs=P("pp", "ep", None),
        check_vma=False,
    )
```
